32 devices in a mesh: elem: 8 (over y, x, core), band: 4 (over z).
Axes of the slice: x: 2, y: 2, z: 4, core: 2. Of those that a mesh axis runs over, the one named last changes fastest.
Arguments:
- orbitals: bfloat16 [8, 512, 13824], P('elem', 'band'), may hold values from -6 to 6
- potential: float32 [8, 13824], P('elem'), may hold values from 0 to 1.9
- basis_count: int32 [8], P('elem'), may hold values from 256 to 512, as said below
- states: bfloat16 [8, 512, 512], P('elem', None, 'band'), may hold values from -6 to 6
Outputs:
- filtered_states: bfloat16 [8, 512, 512], P('elem', None, 'band')
The draws below stay inside these ranges and needn't reach their ends.
Inputs may be any that keep to these rules, and one draw needn't show every extreme that they name: `basis_count`: some element keeps all 512 basis functions and some element keeps 512 // 2 of them in every draw.
All inputs are finite; a program needn't handle non-finite values.
Results may differ from the reference program's by a relative error of at most 0.03.
Values may be sent and summed in bfloat16 or wider, within the bound.
A program may use at most 64 MiB of HBM per device.

```python
from functools import partial
import jax
import jax.numpy as jnp
from jax import lax

NB = 512
P_SIZE = 24
G = 13824
DEG = 2
EB = 4
NS = 512
ELEMS = 8
N_BAND = 4


def draw_basis_count(key, part):
    first_key, second_key = jax.random.split(key)
    counts = jax.random.randint(first_key, (ELEMS,), NB // 2, NB + 1, dtype=jnp.int32)
    shuffled = jax.random.permutation(second_key, ELEMS)
    counts = counts.at[shuffled[0]].set(NB)
    counts = counts.at[shuffled[1]].set(NB // 2)
    return counts


def level_of(stream_key, dims, cuts, low, high):
    def one(axis_at, parts):
        steps = jax.random.uniform(jax.random.fold_in(jax.random.fold_in(stream_key, 6), axis_at), (parts,), jnp.float32, low / len(cuts), high / len(cuts))
        return jnp.repeat(jnp.exp(steps), dims[axis_at] // parts).reshape((-1,) + (1,) * (len(dims) - axis_at - 1))

    level = one(*cuts[0])
    for cut in cuts[1:]:
        level = level * one(*cut)
    return level


def centred(stream_key, dims, width, reach, shards=(), kind=jnp.bfloat16):
    result = width * jax.random.normal(stream_key, dims, jnp.float32)
    if shards:
        result = result * level_of(stream_key, dims, shards, -0.22, 0.18)
    return jnp.clip(result, -reach, reach).astype(kind)


def setup_inputs(seed: int = 0) -> dict:
    key_list = jax.random.split(jax.random.key(seed), 5)
    orbitals = centred(key_list[0], (ELEMS, NB, G), 1.0, 6.0, ((0, 8), (1, 4)))
    potential = jnp.clip(1.9 * jax.random.uniform(key_list[1], (ELEMS, G), jnp.float32) ** level_of(key_list[1], (ELEMS, G), ((0, 8),), -0.2, 0.2), 0.0, 1.9)
    basis_count = draw_basis_count(jax.random.fold_in(key_list[4], 71), 0)
    states = centred(key_list[3], (ELEMS, NB, NS), 1.0, 6.0, ((0, 8), (2, 4)))
    return dict(orbitals=orbitals, potential=potential, basis_count=basis_count, states=states)


LOW_EDGE = 4.0
HIGH_EDGE = 14.0
PENALTY = 1.0
SHIFT_CENTER = 4.0
HALF_WIDTH = 6.0
HIGHEST = lax.Precision.HIGHEST

def laplace_apply(values):
    padded = jnp.pad(values, ((0, 0), (1, 1), (1, 1), (1, 1)))
    beside = padded[:, 2:, 1:-1, 1:-1] + padded[:, :-2, 1:-1, 1:-1]
    beside = beside + padded[:, 1:-1, 2:, 1:-1] + padded[:, 1:-1, :-2, 1:-1]
    beside = beside + padded[:, 1:-1, 1:-1, 2:] + padded[:, 1:-1, 1:-1, :-2]
    return 6.0 * values - beside

def hamiltonian(values, potential):
    return laplace_apply(values) + potential * values

def filtered(orbitals, potential, kept_count, start_index):
    orbital_count = orbitals.shape[0]
    layout = (orbital_count, P_SIZE, P_SIZE, P_SIZE)
    cube_potential = potential.reshape(P_SIZE, P_SIZE, P_SIZE)
    middle = 0.5 * (HIGH_EDGE + LOW_EDGE)
    spread = 0.5 * (HIGH_EDGE - LOW_EDGE)
    previous = orbitals.astype(jnp.float32).reshape(layout)
    current = (hamiltonian(previous, cube_potential) - middle * previous) / spread
    for repeat in range(DEG - 1):
        following = 2.0 * (hamiltonian(current, cube_potential) - middle * current) / spread - previous
        previous, current = (current, following)
    magnitude = jnp.sqrt(lax.optimization_barrier(jnp.mean(current * current, axis=(1, 2, 3), keepdims=True)) + 1e-06)
    active = start_index + jnp.arange(orbital_count, dtype=jnp.int32) < kept_count
    basis = jnp.where(active[:, None, None, None], current / magnitude, 0.0).astype(jnp.bfloat16)
    applied = hamiltonian(basis.astype(jnp.float32), cube_potential).astype(jnp.bfloat16)
    return (basis.reshape(orbital_count, -1), applied.reshape(orbital_count, -1))

def face_pair(gridded, axis_place, upper):
    extent = gridded.shape[axis_place]
    surface = lax.index_in_dim(gridded, extent - 1 if upper else 0, axis_place, keepdims=False)
    beneath = lax.index_in_dim(gridded, extent - 2 if upper else 1, axis_place, keepdims=False)
    return (surface, beneath)

def face_terms(own_surface, own_beneath, other_surface, other_beneath):
    own_slope = own_surface - own_beneath
    other_slope = other_surface - other_beneath
    leading = jnp.concatenate([-PENALTY * own_surface + 0.5 * own_slope, 0.5 * own_surface], axis=-1)
    trailing = jnp.concatenate([other_surface, other_slope], axis=-1)
    return (leading, trailing)

def filter_one(packed):
    orbitals, potential, kept_count = packed
    return filtered(orbitals, potential, kept_count, 0)

def element_blocks(basis_all, applied_all, element):
    directions = [(1, 1, True, False), (-1, 1, False, True), (EB, 0, True, False), (-EB, 0, False, True)]
    planes = P_SIZE // N_BAND
    own = basis_all[element].astype(jnp.float32).reshape(NB, N_BAND, planes, P_SIZE, P_SIZE)
    own_applied = applied_all[element].astype(jnp.float32).reshape(NB, N_BAND, -1)
    interior = jnp.einsum('asg,bsg->sab', own.reshape(NB, N_BAND, -1), own_applied, precision=HIGHEST) * (1.0 / G)
    partials = [interior]
    for offset, axis_code, own_upper, other_upper in directions:
        neighbour = (element + offset) % ELEMS
        other = basis_all[neighbour].astype(jnp.float32).reshape(NB, N_BAND, planes, P_SIZE, P_SIZE)
        own_surface, own_beneath = face_pair(own, 3 + axis_code, own_upper)
        other_surface, other_beneath = face_pair(other, 3 + axis_code, other_upper)
        leading, trailing = face_terms(own_surface.reshape(NB, N_BAND, -1), own_beneath.reshape(NB, N_BAND, -1), other_surface.reshape(NB, N_BAND, -1), other_beneath.reshape(NB, N_BAND, -1))
        partials.append(jnp.einsum('asf,bsf->sab', leading, trailing, precision=HIGHEST) * (1.0 / (P_SIZE * P_SIZE)))
    stacked = jnp.stack(partials)
    rounded = lax.optimization_barrier(stacked.astype(jnp.bfloat16)).astype(jnp.float32)
    return lax.optimization_barrier(jnp.sum(rounded, axis=1)).astype(jnp.bfloat16)

def apply_all(blocks, current):
    offsets = [0, 1, -1, EB, -EB]

    def one_element(element):
        running = jnp.zeros((NB, current.shape[2]), jnp.float32)
        for position, offset in enumerate(offsets):
            source = current[(element + offset) % ELEMS]
            running = running + jnp.dot(blocks[element, position].astype(jnp.float32), source.astype(jnp.float32), preferred_element_type=jnp.float32)
        return running
    return lax.map(one_element, jnp.arange(ELEMS, dtype=jnp.int32))

def scaled(blocks, current):
    return (apply_all(blocks, current) - SHIFT_CENTER * current.astype(jnp.float32)) / HALF_WIDTH

def reference(orbitals, potential, basis_count, states):
    basis_all, applied_all = lax.map(filter_one, (orbitals, potential, basis_count))
    blocks = lax.map(partial(element_blocks, basis_all, applied_all), jnp.arange(ELEMS, dtype=jnp.int32))
    first_term = scaled(blocks, states).astype(jnp.bfloat16)
    second_term = (2.0 * scaled(blocks, first_term) - states.astype(jnp.float32)).astype(jnp.bfloat16)
    third_term = 2.0 * scaled(blocks, second_term) - first_term.astype(jnp.float32)
    magnitude = jnp.sqrt(lax.optimization_barrier(jnp.mean(third_term * third_term, axis=1, keepdims=True)) + 1e-06)
    return (third_term / magnitude).astype(jnp.bfloat16)
```

```python
import functools

import jax
import jax.numpy as jnp
from jax import lax
from jax.experimental import pallas as pl
from jax.experimental.pallas import tpu as pltpu
from jax.sharding import PartitionSpec as P

P_SIZE = 24
G = 13824
EB = 4
PLANE = P_SIZE * P_SIZE
PAD = 640
ROWS = 16


LOW_EDGE = 4.0
HIGH_EDGE = 14.0
SHIFT_CENTER = 4.0
HALF_WIDTH = 6.0
VMEM_LIMIT = 48 * 1024 * 1024
NT = (((1,), (1,)), ((), ()))


def from_behind(value, axis, by):
    devices = lax.axis_size(axis)
    return lax.ppermute(value, axis, [(i, (i + by) % devices) for i in range(devices)])


def side_masks(length):
    where = jnp.arange(length, dtype=jnp.int32)
    zpos = where % P_SIZE
    ypos = where // P_SIZE % P_SIZE
    return jnp.stack(
        [
            (zpos < P_SIZE - 1).astype(jnp.float32),
            (zpos > 0).astype(jnp.float32),
            (ypos < P_SIZE - 1).astype(jnp.float32),
            (ypos > 0).astype(jnp.float32),
        ]
    )


def lane_chunks(length):
    step = 1152
    return [(at, min(step, length - at)) for at in range(0, length, step)]


def neighbour_sum(ref, masks_ref, at, size):
    base = PAD + at

    def shifted(by):
        return ref[:, base + by : base + by + size]

    def mask(which):
        return masks_ref[which : which + 1, at : at + size]

    total = shifted(PLANE) + shifted(-PLANE)
    total = total + mask(0) * shifted(1) + mask(1) * shifted(-1)
    return total + mask(2) * shifted(P_SIZE) + mask(3) * shifted(-P_SIZE)


def clear_pads(ref, length):
    ref[:, 0:PAD] = jnp.zeros((ref.shape[0], PAD), jnp.float32)
    ref[:, PAD + length :] = jnp.zeros((ref.shape[0], ref.shape[1] - PAD - length), jnp.float32)


def filter_kernel(slabs, bounds_ref, orbitals_ref, diag_ref, masks_ref, out_ref, first_ref, second_ref):
    spread = 0.5 * (HIGH_EDGE - LOW_EDGE)
    rows, length = orbitals_ref.shape

    @pl.when(pl.program_id(0) == 0)
    def _():
        clear_pads(first_ref, length)
        clear_pads(second_ref, length)

    first_ref[:, PAD : PAD + length] = orbitals_ref[...].astype(jnp.float32)
    for at, size in lane_chunks(length):
        diag = diag_ref[0:1, at : at + size]
        own = first_ref[:, PAD + at : PAD + at + size]
        second_ref[:, PAD + at : PAD + at + size] = diag * own - neighbour_sum(
            first_ref, masks_ref, at, size
        ) * (1.0 / spread)
    squares = jnp.zeros((rows, 1), jnp.float32)
    for at, size in lane_chunks(length):
        diag = diag_ref[0:1, at : at + size]
        own = second_ref[:, PAD + at : PAD + at + size]
        previous = first_ref[:, PAD + at : PAD + at + size]
        value = (
            2.0 * diag * own
            - neighbour_sum(second_ref, masks_ref, at, size) * (2.0 / spread)
            - previous
        )
        first_ref[:, PAD + at : PAD + at + size] = value
        squares = squares + jnp.sum(value * value, axis=1, keepdims=True)
    scale = 1.0 / jnp.sqrt(squares * (1.0 / length) + 1e-06)
    row = bounds_ref[1] + pl.program_id(0) * rows + lax.broadcasted_iota(jnp.int32, (rows, 1), 0)
    scale = jnp.where(row < bounds_ref[0], scale, 0.0)
    share = length // slabs
    for slab in range(slabs):
        start = PAD + slab * share
        out_ref[slab] = (first_ref[:, start : start + share] * scale).astype(jnp.bfloat16)


def filtered_basis(orbitals, potential, kept_count, start_index, slabs):
    count, length = orbitals.shape
    middle = 0.5 * (HIGH_EDGE + LOW_EDGE)
    spread = 0.5 * (HIGH_EDGE - LOW_EDGE)
    diag = ((6.0 - middle) + potential)[None] / spread
    bounds = jnp.stack([kept_count, start_index]).astype(jnp.int32)
    return pl.pallas_call(
        functools.partial(filter_kernel, slabs),
        grid=(count // ROWS,),
        in_specs=[
            pl.BlockSpec(memory_space=pltpu.SMEM),
            pl.BlockSpec((ROWS, length), lambda i: (i, 0)),
            pl.BlockSpec((1, length), lambda i: (0, 0)),
            pl.BlockSpec((4, length), lambda i: (0, 0)),
        ],
        out_specs=pl.BlockSpec((slabs, ROWS, length // slabs), lambda i: (0, i, 0)),
        out_shape=jax.ShapeDtypeStruct((slabs, count, length // slabs), jnp.bfloat16),
        scratch_shapes=[pltpu.VMEM((ROWS, length + 2 * PAD), jnp.float32)] * 2,
        compiler_params=pltpu.CompilerParams(vmem_limit_bytes=VMEM_LIMIT),
    )(bounds, orbitals, diag, side_masks(length))


def face_chunk(length):
    return 1152 if length % 1152 == 0 else length


def face_selector(chunk):
    points = chunk // P_SIZE
    group = (2 * points + 127) // 128 * 128
    where = jnp.arange(chunk, dtype=jnp.int32)[:, None]
    zpos, ypos, xpos = where % P_SIZE, where // P_SIZE % P_SIZE, where // PLANE
    column = jnp.arange(group, dtype=jnp.int32)[None]
    point, late = column % points, column >= points
    used = column < 2 * points
    top = P_SIZE - 1
    layers = [(top - 1, top), (0, 1)]
    parts = []
    for pos, spot in ((zpos, where // P_SIZE), (ypos, xpos * P_SIZE + zpos)):
        for early_layer, late_layer in layers:
            layer = jnp.where(late, late_layer, early_layer)
            parts.append(((spot == point) & (pos == layer) & used).astype(jnp.bfloat16))
    return jnp.concatenate(parts, axis=1)


def faces_kernel(rows_ref, select_ref, lz_ref, rz_ref, ly_ref, ry_ref):
    chunk = select_ref.shape[0]
    group = select_ref.shape[1] // 4
    for which in range(rows_ref.shape[1] // chunk):
        picked = jnp.dot(
            rows_ref[:, which * chunk : (which + 1) * chunk],
            select_ref[...],
            preferred_element_type=jnp.float32,
        ).astype(jnp.bfloat16)
        for place, out in enumerate((lz_ref, rz_ref, ly_ref, ry_ref)):
            out[:, which * group : (which + 1) * group] = picked[:, place * group : (place + 1) * group]


def face_layers(rows):
    count, length = rows.shape
    chunk = face_chunk(length)
    select = face_selector(chunk)
    width = length // chunk * (select.shape[1] // 4)
    step = count // 4
    return pl.pallas_call(
        faces_kernel,
        grid=(4,),
        in_specs=[
            pl.BlockSpec((step, length), lambda i: (i, 0)),
            pl.BlockSpec(select.shape, lambda i: (0, 0)),
        ],
        out_specs=[pl.BlockSpec((step, width), lambda i: (i, 0))] * 4,
        out_shape=[jax.ShapeDtypeStruct((count, width), jnp.bfloat16)] * 4,
        compiler_params=pltpu.CompilerParams(vmem_limit_bytes=VMEM_LIMIT),
    )(rows, select)


def interior_kernel(all_ref, rows_ref, diag_ref, masks_ref, out_ref, wide_ref, applied_ref):
    count, length = rows_ref.shape

    @pl.when(pl.program_id(0) == 0)
    def _():
        clear_pads(wide_ref, length)

    @pl.loop(0, count // ROWS)
    def _(block):
        here = pl.ds(pl.multiple_of(block * ROWS, ROWS), ROWS)
        wide_ref[:, PAD : PAD + length] = rows_ref[here, :].astype(jnp.float32)
        for at, size in lane_chunks(length):
            own = wide_ref[:, PAD + at : PAD + at + size]
            applied_ref[here, at : at + size] = (
                diag_ref[0:1, at : at + size] * own - neighbour_sum(wide_ref, masks_ref, at, size)
            ).astype(jnp.bfloat16)

    out_ref[...] = lax.dot_general(
        applied_ref[...], all_ref[...], NT, preferred_element_type=jnp.float32
    )


def interior_block(rows, slab_potential):
    count, length = rows.shape
    step = count // 4
    return pl.pallas_call(
        interior_kernel,
        grid=(4,),
        in_specs=[
            pl.BlockSpec((count, length), lambda i: (0, 0)),
            pl.BlockSpec((step, length), lambda i: (i, 0)),
            pl.BlockSpec((1, length), lambda i: (0, 0)),
            pl.BlockSpec((4, length), lambda i: (0, 0)),
        ],
        out_specs=pl.BlockSpec((step, count), lambda i: (i, 0)),
        out_shape=jax.ShapeDtypeStruct((count, count), jnp.float32),
        scratch_shapes=[
            pltpu.VMEM((ROWS, length + 2 * PAD), jnp.float32),
            pltpu.VMEM((step, length), jnp.bfloat16),
        ],
        compiler_params=pltpu.CompilerParams(vmem_limit_bytes=VMEM_LIMIT),
    )(rows, rows, (6.0 + slab_potential)[None], side_masks(length))


def partials_kernel(inner_ref, near_ref, far_ref, lz_ref, rz_ref, ly_ref, ry_ref, out_ref):
    def product(a, b):
        return lax.dot_general(a, b, NT, preferred_element_type=jnp.float32)

    half = PLANE // 2
    seam = product(near_ref[...], far_ref[...])
    out_ref[0] = ((inner_ref[...] - seam) * (1.0 / G)).astype(jnp.bfloat16)
    weight = -0.5 / PLANE
    out_ref[1] = (product(lz_ref[...], rz_ref[...]) * weight).astype(jnp.bfloat16)
    out_ref[2] = (product(ly_ref[...], ry_ref[...]) * weight).astype(jnp.bfloat16)


def partial_blocks(inner, near, far, lz, rz, ly, ry):
    count = inner.shape[0]
    step = count // 4

    def cut(value):
        return pl.BlockSpec((step, value.shape[1]), lambda i: (i, 0))

    def full(value):
        return pl.BlockSpec(value.shape, lambda i: (0, 0))

    return pl.pallas_call(
        partials_kernel,
        grid=(4,),
        in_specs=[cut(inner), cut(near), full(far), cut(lz), full(rz), cut(ly), full(ry)],
        out_specs=pl.BlockSpec((3, step, count), lambda i: (0, i, 0)),
        out_shape=jax.ShapeDtypeStruct((3, count, count), jnp.bfloat16),
        compiler_params=pltpu.CompilerParams(vmem_limit_bytes=VMEM_LIMIT),
    )(inner, near, far, lz, rz, ly, ry)


def apply_blocks(terms, current):
    offsets = [0, 1, -1, EB, -EB]
    running = jnp.zeros((terms[0][0].shape[0], current.shape[1]), jnp.float32)
    for position, offset in enumerate(offsets):
        matrix, contract = terms[position]
        if offset == 0:
            source = current
        else:
            source = from_behind(current, "elem", -offset)
        running = running + lax.dot_general(
            matrix, source, (((contract,), (0,)), ((), ())), preferred_element_type=jnp.float32
        )
    return running


def scaled(terms, current):
    return (apply_blocks(terms, current) - SHIFT_CENTER * current.astype(jnp.float32)) / HALF_WIDTH


def summed_blocks(partials):
    return lax.psum(partials, "band")


def on_device(orbitals, potential, basis_count, states):
    per_device = orbitals.shape[1]
    slabs = lax.axis_size("band")
    band_place = lax.axis_index("band")
    start_index = band_place * per_device
    basis = filtered_basis(orbitals[0], potential[0], basis_count[0], start_index, slabs)
    basis_rows = lax.all_to_all(basis, "band", split_axis=0, concat_axis=0, tiled=True)
    basis_rows = basis_rows.reshape(slabs * per_device, -1)
    slab_length = basis_rows.shape[1]
    slab_potential = lax.dynamic_slice_in_dim(
        potential[0], band_place * slab_length, slab_length, 0
    )
    half = PLANE // 2
    initial, last = basis_rows[:, :PLANE], basis_rows[:, slab_length - PLANE :]
    up = [(i, i + 1) for i in range(slabs - 1)]
    down = [(j, i) for i, j in up]
    after = lax.ppermute(initial[:, :half], "band", down)
    before = lax.ppermute(last[:, half:], "band", up)
    lz, rz, ly, ry = face_layers(basis_rows)
    rz = from_behind(rz, "elem", -1)
    ry = from_behind(ry, "elem", -EB)
    inner = interior_block(basis_rows, slab_potential)
    near = jnp.concatenate([last[:, :half], after, initial[:, half:], before], axis=1)
    far = jnp.concatenate([after, last[:, :half], before, initial[:, half:]], axis=1)
    partials = partial_blocks(inner, near, far, lz, rz, ly, ry)
    summed = summed_blocks(partials)
    mirrored = []
    for position, offset in ((1, 1), (2, EB)):
        mirrored.append(from_behind(summed[position], "elem", offset))
    terms = [(summed[0], 1), (summed[1], 1), (mirrored[0], 0), (summed[2], 1), (mirrored[1], 0)]
    start_states = states[0]
    first_term = scaled(terms, start_states).astype(jnp.bfloat16)
    second_term = (2.0 * scaled(terms, first_term) - start_states.astype(jnp.float32)).astype(
        jnp.bfloat16
    )
    third_term = 2.0 * scaled(terms, second_term) - first_term.astype(jnp.float32)
    magnitude = jnp.sqrt(jnp.mean(third_term * third_term, axis=0, keepdims=True) + 1e-06)
    return (third_term / magnitude).astype(jnp.bfloat16)[None]


def solution(mesh):
    placed = (P("elem", "band", None), P("elem", None), P("elem"), P("elem", None, "band"))
    return jax.shard_map(
        on_device, mesh=mesh, in_specs=placed, out_specs=P("elem", None, "band"), check_vma=False
    )
```

```python
import functools

import jax
import jax.numpy as jnp
from jax import lax
from jax.experimental import pallas as pl
from jax.experimental.pallas import tpu as pltpu
from jax.sharding import PartitionSpec as P
import ml_dtypes
import numpy as np

P_SIZE = 24
G = 13824
EB = 4
PLANE = P_SIZE * P_SIZE
PAD = 640
TILE = 256
PERIOD = 9
SPANS = ((-640, -256), (-128, 384), (512, 896))


LOW_EDGE = 4.0
HIGH_EDGE = 14.0
SHIFT_CENTER = 4.0
HALF_WIDTH = 6.0
VMEM_LIMIT = 48 * 1024 * 1024
NT = (((1,), (1,)), ((), ()))


def from_behind(value, axis, by):
    devices = lax.axis_size(axis)
    return lax.ppermute(value, axis, [(i, (i + by) % devices) for i in range(devices)])


def stencil_tables():
    tables = []
    source = np.concatenate([np.arange(*span) for span in SPANS])[:, None]
    for which in range(PERIOD):
        column = np.arange(TILE)[None]
        zpos = (which * TILE + column) % P_SIZE
        ypos = (which * TILE + column) // P_SIZE % P_SIZE
        hit = (source == column + PLANE) | (source == column - PLANE)
        hit = hit | ((source == column + 1) & (zpos < P_SIZE - 1))
        hit = hit | ((source == column - 1) & (zpos > 0))
        hit = hit | ((source == column + P_SIZE) & (ypos < P_SIZE - 1))
        hit = hit | ((source == column - P_SIZE) & (ypos > 0))
        tables.append(hit)
    return jnp.asarray(np.stack(tables).astype(ml_dtypes.bfloat16))


def padded_width(length):
    return 2 * PAD + (length + TILE - 1) // TILE * TILE


def windows(ref, at):
    parts = []
    for low, high in SPANS:
        start = PAD + at + low
        if not isinstance(at, int):
            start = pl.multiple_of(start, 128)
        parts.append(ref[:, pl.ds(start, high - low)])
    return jnp.concatenate(parts, axis=1)


def clear_pads(ref, length):
    ref[:, 0:PAD] = jnp.zeros((ref.shape[0], PAD), ref.dtype)
    inner = PAD + length // 128 * 128
    ref[:, inner:] = jnp.zeros((ref.shape[0], ref.shape[1] - inner), ref.dtype)


def filter_kernel(slabs, bounds_ref, orbitals_ref, diag_ref, table_ref, out_ref, low_ref, mid_ref, wide_ref):
    spread = 0.5 * (HIGH_EDGE - LOW_EDGE)
    rows, length = orbitals_ref.shape
    turn = PERIOD * TILE
    repeats = length // turn
    clear_pads(low_ref, length)
    clear_pads(mid_ref, length)
    low_ref[:, PAD : PAD + length] = orbitals_ref[...]

    def sums(ref, which):
        offset = which * TILE
        left = jnp.concatenate([windows(ref, offset + turn * r) for r in range(repeats)], axis=0)
        return jnp.dot(left, table_ref[which], preferred_element_type=jnp.float32)

    def tile_at(which, r):
        return pl.multiple_of(which * TILE + turn * r, TILE)

    @pl.loop(0, PERIOD)
    def _(which):
        total = sums(low_ref, which)
        for r in range(repeats):
            at = tile_at(which, r)
            value = diag_ref[0:1, pl.ds(at, TILE)] * orbitals_ref[:, pl.ds(at, TILE)].astype(
                jnp.float32
            ) - total[r * rows : (r + 1) * rows] * (1.0 / spread)
            wide_ref[:, pl.ds(at, TILE)] = value
            mid_ref[:, pl.ds(pl.multiple_of(PAD + at, 128), TILE)] = value.astype(jnp.bfloat16)

    def second(which, squares):
        total = sums(mid_ref, which)
        for r in range(repeats):
            at = tile_at(which, r)
            value = (
                2.0 * diag_ref[0:1, pl.ds(at, TILE)] * wide_ref[:, pl.ds(at, TILE)]
                - total[r * rows : (r + 1) * rows] * (2.0 / spread)
                - orbitals_ref[:, pl.ds(at, TILE)].astype(jnp.float32)
            )
            wide_ref[:, pl.ds(at, TILE)] = value
            squares = squares + value * value
        return squares

    squares = lax.fori_loop(0, PERIOD, second, jnp.zeros((rows, TILE), jnp.float32))
    squares = jnp.sum(squares, axis=1, keepdims=True)
    scale = 1.0 / jnp.sqrt(squares * (1.0 / length) + 1e-06)
    row = bounds_ref[1] + lax.broadcasted_iota(jnp.int32, (rows, 1), 0)
    scale = jnp.where(row < bounds_ref[0], scale, 0.0)
    share = length // slabs
    for slab in range(slabs):
        out_ref[slab] = (wide_ref[:, slab * share : (slab + 1) * share] * scale).astype(jnp.bfloat16)


def filtered_basis(orbitals, potential, kept_count, start_index, slabs, table):
    count, length = orbitals.shape
    middle = 0.5 * (HIGH_EDGE + LOW_EDGE)
    spread = 0.5 * (HIGH_EDGE - LOW_EDGE)
    diag = ((6.0 - middle) + potential)[None] / spread
    bounds = jnp.stack([kept_count, start_index]).astype(jnp.int32)
    whole = pl.BlockSpec(memory_space=pltpu.VMEM)
    return pl.pallas_call(
        functools.partial(filter_kernel, slabs),
        in_specs=[pl.BlockSpec(memory_space=pltpu.SMEM), whole, whole, whole],
        out_specs=whole,
        out_shape=jax.ShapeDtypeStruct((slabs, count, length // slabs), jnp.bfloat16),
        scratch_shapes=[
            pltpu.VMEM((count, padded_width(length)), jnp.bfloat16),
            pltpu.VMEM((count, padded_width(length)), jnp.bfloat16),
            pltpu.VMEM((count, length), jnp.float32),
        ],
        compiler_params=pltpu.CompilerParams(vmem_limit_bytes=VMEM_LIMIT),
    )(bounds, orbitals, diag, table)


def face_chunk(length):
    return 1152 if length % 1152 == 0 else length


def face_selector(chunk):
    points = chunk // P_SIZE
    group = (2 * points + 127) // 128 * 128
    where = np.arange(chunk)[:, None]
    zpos, ypos, xpos = where % P_SIZE, where // P_SIZE % P_SIZE, where // PLANE
    column = np.arange(group)[None]
    point, late = column % points, column >= points
    used = column < 2 * points
    top = P_SIZE - 1
    layers = [(top - 1, top), (0, 1)]
    parts = []
    for pos, spot in ((zpos, where // P_SIZE), (ypos, xpos * P_SIZE + zpos)):
        for early_layer, late_layer in layers:
            layer = np.where(late, late_layer, early_layer)
            parts.append(((spot == point) & (pos == layer) & used))
    return jnp.asarray(np.concatenate(parts, axis=1).astype(ml_dtypes.bfloat16))


def faces_kernel(rows_ref, select_ref, lz_ref, rz_ref, ly_ref, ry_ref):
    chunk = select_ref.shape[0]
    group = select_ref.shape[1] // 4
    for which in range(rows_ref.shape[1] // chunk):
        picked = jnp.dot(
            rows_ref[:, which * chunk : (which + 1) * chunk],
            select_ref[...],
            preferred_element_type=jnp.float32,
        ).astype(jnp.bfloat16)
        for place, out in enumerate((lz_ref, rz_ref, ly_ref, ry_ref)):
            out[:, which * group : (which + 1) * group] = picked[:, place * group : (place + 1) * group]


def face_layers(rows):
    count, length = rows.shape
    chunk = face_chunk(length)
    select = face_selector(chunk)
    width = length // chunk * (select.shape[1] // 4)
    step = count // 4
    return pl.pallas_call(
        faces_kernel,
        grid=(4,),
        in_specs=[
            pl.BlockSpec((step, length), lambda i: (i, 0)),
            pl.BlockSpec(select.shape, lambda i: (0, 0)),
        ],
        out_specs=[pl.BlockSpec((step, width), lambda i: (i, 0))] * 4,
        out_shape=[jax.ShapeDtypeStruct((count, width), jnp.bfloat16)] * 4,
        compiler_params=pltpu.CompilerParams(vmem_limit_bytes=VMEM_LIMIT),
    )(rows, select)


def interior_kernel(all_ref, rows_ref, diag_ref, table_ref, out_ref, wide_ref, applied_ref):
    count, length = rows_ref.shape
    clear_pads(wide_ref, length)
    wide_ref[:, PAD : PAD + length] = rows_ref[...]
    for at in range(0, length, TILE):
        size = min(TILE, length - at)
        total = jnp.dot(
            windows(wide_ref, at), table_ref[at // TILE % PERIOD], preferred_element_type=jnp.float32
        )
        applied_ref[:, at : at + size] = (
            diag_ref[0:1, at : at + size] * rows_ref[:, at : at + size].astype(jnp.float32)
            - total[:, :size]
        ).astype(jnp.bfloat16)
    out_ref[...] = lax.dot_general(
        applied_ref[...], all_ref[...], NT, preferred_element_type=jnp.float32
    )


def interior_block(rows, slab_potential, table):
    count, length = rows.shape
    step = count // 2
    return pl.pallas_call(
        interior_kernel,
        grid=(2,),
        in_specs=[
            pl.BlockSpec((count, length), lambda i: (0, 0)),
            pl.BlockSpec((step, length), lambda i: (i, 0)),
            pl.BlockSpec((1, length), lambda i: (0, 0)),
            pl.BlockSpec(table.shape, lambda i: (0, 0, 0)),
        ],
        out_specs=pl.BlockSpec((step, count), lambda i: (i, 0)),
        out_shape=jax.ShapeDtypeStruct((count, count), jnp.float32),
        scratch_shapes=[
            pltpu.VMEM((step, padded_width(length)), jnp.bfloat16),
            pltpu.VMEM((step, length), jnp.bfloat16),
        ],
        compiler_params=pltpu.CompilerParams(vmem_limit_bytes=VMEM_LIMIT),
    )(rows, rows, (6.0 + slab_potential)[None], table)


def partials_kernel(inner_ref, near_ref, far_ref, lz_ref, rz_ref, ly_ref, ry_ref, out_ref):
    def product(a, b):
        return lax.dot_general(a, b, NT, preferred_element_type=jnp.float32)

    seam = product(near_ref[...], far_ref[...])
    out_ref[0] = ((inner_ref[...] - seam) * (1.0 / G)).astype(jnp.bfloat16)
    weight = -0.5 / PLANE
    out_ref[1] = (product(lz_ref[...], rz_ref[...]) * weight).astype(jnp.bfloat16)
    out_ref[2] = (product(ly_ref[...], ry_ref[...]) * weight).astype(jnp.bfloat16)


def partial_blocks(inner, near, far, lz, rz, ly, ry):
    count = inner.shape[0]
    step = count // 4

    def cut(value):
        return pl.BlockSpec((step, value.shape[1]), lambda i: (i, 0))

    def full(value):
        return pl.BlockSpec(value.shape, lambda i: (0, 0))

    return pl.pallas_call(
        partials_kernel,
        grid=(4,),
        in_specs=[cut(inner), cut(near), full(far), cut(lz), full(rz), cut(ly), full(ry)],
        out_specs=pl.BlockSpec((3, step, count), lambda i: (0, i, 0)),
        out_shape=jax.ShapeDtypeStruct((3, count, count), jnp.bfloat16),
        compiler_params=pltpu.CompilerParams(vmem_limit_bytes=VMEM_LIMIT),
    )(inner, near, far, lz, rz, ly, ry)


def apply_blocks(terms, current):
    offsets = [0, 1, -1, EB, -EB]
    running = jnp.zeros((terms[0][0].shape[0], current.shape[1]), jnp.float32)
    for position, offset in enumerate(offsets):
        matrix, contract = terms[position]
        if offset == 0:
            source = current
        else:
            source = from_behind(current, "elem", -offset)
        running = running + lax.dot_general(
            matrix, source, (((contract,), (0,)), ((), ())), preferred_element_type=jnp.float32
        )
    return running


def scaled(terms, current):
    return (apply_blocks(terms, current) - SHIFT_CENTER * current.astype(jnp.float32)) / HALF_WIDTH


def summed_blocks(partials):
    return lax.psum(partials, "band")


def on_device(orbitals, potential, basis_count, states):
    per_device = orbitals.shape[1]
    slabs = lax.axis_size("band")
    band_place = lax.axis_index("band")
    table = stencil_tables()
    start_index = band_place * per_device
    basis = filtered_basis(orbitals[0], potential[0], basis_count[0], start_index, slabs, table)
    basis_rows = lax.all_to_all(basis, "band", split_axis=0, concat_axis=0, tiled=True)
    basis_rows = basis_rows.reshape(slabs * per_device, -1)
    slab_length = basis_rows.shape[1]
    slab_potential = lax.dynamic_slice_in_dim(
        potential[0], band_place * slab_length, slab_length, 0
    )
    half = PLANE // 2
    initial, last = basis_rows[:, :PLANE], basis_rows[:, slab_length - PLANE :]
    up = [(i, i + 1) for i in range(slabs - 1)]
    down = [(j, i) for i, j in up]
    after = lax.ppermute(initial[:, :half], "band", down)
    before = lax.ppermute(last[:, half:], "band", up)
    lz, rz, ly, ry = face_layers(basis_rows)
    rz = from_behind(rz, "elem", -1)
    ry = from_behind(ry, "elem", -EB)
    inner = interior_block(basis_rows, slab_potential, table)
    near = jnp.concatenate([last[:, :half], after, initial[:, half:], before], axis=1)
    far = jnp.concatenate([after, last[:, :half], before, initial[:, half:]], axis=1)
    partials = partial_blocks(inner, near, far, lz, rz, ly, ry)
    summed = summed_blocks(partials)
    mirrored = []
    for position, offset in ((1, 1), (2, EB)):
        mirrored.append(from_behind(summed[position], "elem", offset))
    terms = [(summed[0], 1), (summed[1], 1), (mirrored[0], 0), (summed[2], 1), (mirrored[1], 0)]
    start_states = states[0]
    first_term = scaled(terms, start_states).astype(jnp.bfloat16)
    second_term = (2.0 * scaled(terms, first_term) - start_states.astype(jnp.float32)).astype(
        jnp.bfloat16
    )
    third_term = 2.0 * scaled(terms, second_term) - first_term.astype(jnp.float32)
    magnitude = jnp.sqrt(jnp.mean(third_term * third_term, axis=0, keepdims=True) + 1e-06)
    return (third_term / magnitude).astype(jnp.bfloat16)[None]


def solution(mesh):
    placed = (P("elem", "band", None), P("elem", None), P("elem"), P("elem", None, "band"))
    return jax.shard_map(
        on_device, mesh=mesh, in_specs=placed, out_specs=P("elem", None, "band"), check_vma=False
    )
```

```python
import functools

import jax
import jax.numpy as jnp
from jax import lax
from jax.experimental import pallas as pl
from jax.experimental.pallas import tpu as pltpu
from jax.sharding import PartitionSpec as P
import ml_dtypes
import numpy as np

P_SIZE = 24
G = 13824
EB = 4
PLANE = P_SIZE * P_SIZE
PAD = 640
TILE = 256
PERIOD = 9
SPANS = ((-640, -256), (-128, 384), (512, 896))


LOW_EDGE = 4.0
HIGH_EDGE = 14.0
SHIFT_CENTER = 4.0
HALF_WIDTH = 6.0
VMEM_LIMIT = 48 * 1024 * 1024
NT = (((1,), (1,)), ((), ()))


def from_behind(value, axis, by):
    devices = lax.axis_size(axis)
    return lax.ppermute(value, axis, [(i, (i + by) % devices) for i in range(devices)])


def stencil_tables():
    tables = []
    source = np.concatenate([np.arange(*span) for span in SPANS])[:, None]
    for which in range(PERIOD):
        column = np.arange(TILE)[None]
        zpos = (which * TILE + column) % P_SIZE
        ypos = (which * TILE + column) // P_SIZE % P_SIZE
        hit = (source == column + PLANE) | (source == column - PLANE)
        hit = hit | ((source == column + 1) & (zpos < P_SIZE - 1))
        hit = hit | ((source == column - 1) & (zpos > 0))
        hit = hit | ((source == column + P_SIZE) & (ypos < P_SIZE - 1))
        hit = hit | ((source == column - P_SIZE) & (ypos > 0))
        tables.append(hit)
    return jnp.asarray(np.stack(tables).astype(ml_dtypes.bfloat16))


def padded_width(length):
    return 2 * PAD + (length + TILE - 1) // TILE * TILE


def windows(ref, at):
    parts = []
    for low, high in SPANS:
        start = PAD + at + low
        if not isinstance(at, int):
            start = pl.multiple_of(start, 128)
        parts.append(ref[:, pl.ds(start, high - low)])
    return jnp.concatenate(parts, axis=1)


def clear_pads(ref, length):
    ref[:, 0:PAD] = jnp.zeros((ref.shape[0], PAD), ref.dtype)
    inner = PAD + length // 128 * 128
    ref[:, inner:] = jnp.zeros((ref.shape[0], ref.shape[1] - inner), ref.dtype)


def filter_kernel(slabs, bounds_ref, orbitals_ref, diag_ref, table_ref, out_ref, low_ref, mid_ref, wide_ref):
    spread = 0.5 * (HIGH_EDGE - LOW_EDGE)
    rows, length = orbitals_ref.shape
    turn = PERIOD * TILE
    repeats = length // turn
    clear_pads(low_ref, length)
    clear_pads(mid_ref, length)
    low_ref[:, PAD : PAD + length] = orbitals_ref[...]

    def sums(ref, which):
        offset = which * TILE
        left = jnp.concatenate([windows(ref, offset + turn * r) for r in range(repeats)], axis=0)
        return jnp.dot(left, table_ref[which], preferred_element_type=jnp.float32)

    def tile_at(which, r):
        return pl.multiple_of(which * TILE + turn * r, TILE)

    @pl.loop(0, PERIOD)
    def _(which):
        total = sums(low_ref, which)
        for r in range(repeats):
            at = tile_at(which, r)
            value = diag_ref[0:1, pl.ds(at, TILE)] * orbitals_ref[:, pl.ds(at, TILE)].astype(
                jnp.float32
            ) - total[r * rows : (r + 1) * rows] * (1.0 / spread)
            wide_ref[:, pl.ds(at, TILE)] = value
            mid_ref[:, pl.ds(pl.multiple_of(PAD + at, 128), TILE)] = value.astype(jnp.bfloat16)

    def second(which, squares):
        total = sums(mid_ref, which)
        for r in range(repeats):
            at = tile_at(which, r)
            value = (
                2.0 * diag_ref[0:1, pl.ds(at, TILE)] * wide_ref[:, pl.ds(at, TILE)]
                - total[r * rows : (r + 1) * rows] * (2.0 / spread)
                - orbitals_ref[:, pl.ds(at, TILE)].astype(jnp.float32)
            )
            wide_ref[:, pl.ds(at, TILE)] = value
            squares = squares + value * value
        return squares

    squares = lax.fori_loop(0, PERIOD, second, jnp.zeros((rows, TILE), jnp.float32))
    squares = jnp.sum(squares, axis=1, keepdims=True)
    scale = 1.0 / jnp.sqrt(squares * (1.0 / length) + 1e-06)
    row = bounds_ref[1] + lax.broadcasted_iota(jnp.int32, (rows, 1), 0)
    scale = jnp.where(row < bounds_ref[0], scale, 0.0)
    share = length // slabs
    for slab in range(slabs):
        out_ref[slab] = (wide_ref[:, slab * share : (slab + 1) * share] * scale).astype(jnp.bfloat16)


def filtered_basis(orbitals, potential, kept_count, start_index, slabs, table):
    count, length = orbitals.shape
    middle = 0.5 * (HIGH_EDGE + LOW_EDGE)
    spread = 0.5 * (HIGH_EDGE - LOW_EDGE)
    diag = ((6.0 - middle) + potential)[None] / spread
    bounds = jnp.stack([kept_count, start_index]).astype(jnp.int32)
    whole = pl.BlockSpec(memory_space=pltpu.VMEM)
    return pl.pallas_call(
        functools.partial(filter_kernel, slabs),
        in_specs=[pl.BlockSpec(memory_space=pltpu.SMEM), whole, whole, whole],
        out_specs=whole,
        out_shape=jax.ShapeDtypeStruct((slabs, count, length // slabs), jnp.bfloat16),
        scratch_shapes=[
            pltpu.VMEM((count, padded_width(length)), jnp.bfloat16),
            pltpu.VMEM((count, padded_width(length)), jnp.bfloat16),
            pltpu.VMEM((count, length), jnp.float32),
        ],
        compiler_params=pltpu.CompilerParams(vmem_limit_bytes=VMEM_LIMIT),
    )(bounds, orbitals, diag, table)


def face_chunk(length):
    return 1152 if length % 1152 == 0 else length


def face_selector(chunk):
    points = chunk // P_SIZE
    group = (2 * points + 127) // 128 * 128
    where = np.arange(chunk)[:, None]
    zpos, ypos, xpos = where % P_SIZE, where // P_SIZE % P_SIZE, where // PLANE
    column = np.arange(group)[None]
    point, late = column % points, column >= points
    used = column < 2 * points
    top = P_SIZE - 1
    layers = [(top - 1, top), (0, 1)]
    parts = []
    for pos, spot in ((zpos, where // P_SIZE), (ypos, xpos * P_SIZE + zpos)):
        for early_layer, late_layer in layers:
            layer = np.where(late, late_layer, early_layer)
            parts.append(((spot == point) & (pos == layer) & used))
    return jnp.asarray(np.concatenate(parts, axis=1).astype(ml_dtypes.bfloat16))


def faces_kernel(rows_ref, select_ref, lz_ref, rz_ref, ly_ref, ry_ref):
    chunk = select_ref.shape[0]
    group = select_ref.shape[1] // 4
    for which in range(rows_ref.shape[1] // chunk):
        picked = jnp.dot(
            rows_ref[:, which * chunk : (which + 1) * chunk],
            select_ref[...],
            preferred_element_type=jnp.float32,
        ).astype(jnp.bfloat16)
        for place, out in enumerate((lz_ref, rz_ref, ly_ref, ry_ref)):
            out[:, which * group : (which + 1) * group] = picked[:, place * group : (place + 1) * group]


def face_layers(rows):
    count, length = rows.shape
    chunk = face_chunk(length)
    select = face_selector(chunk)
    width = length // chunk * (select.shape[1] // 4)
    step = count // 4
    return pl.pallas_call(
        faces_kernel,
        grid=(4,),
        in_specs=[
            pl.BlockSpec((step, length), lambda i: (i, 0)),
            pl.BlockSpec(select.shape, lambda i: (0, 0)),
        ],
        out_specs=[pl.BlockSpec((step, width), lambda i: (i, 0))] * 4,
        out_shape=[jax.ShapeDtypeStruct((count, width), jnp.bfloat16)] * 4,
        compiler_params=pltpu.CompilerParams(vmem_limit_bytes=VMEM_LIMIT),
    )(rows, select)


def interior_kernel(all_ref, rows_ref, diag_ref, table_ref, out_ref, wide_ref, applied_ref):
    count, length = rows_ref.shape
    clear_pads(wide_ref, length)
    wide_ref[:, PAD : PAD + length] = rows_ref[...]
    for at in range(0, length, TILE):
        size = min(TILE, length - at)
        total = jnp.dot(
            windows(wide_ref, at), table_ref[at // TILE % PERIOD], preferred_element_type=jnp.float32
        )
        applied_ref[:, at : at + size] = (
            diag_ref[0:1, at : at + size] * rows_ref[:, at : at + size].astype(jnp.float32)
            - total[:, :size]
        ).astype(jnp.bfloat16)
    out_ref[...] = lax.dot_general(
        applied_ref[...], all_ref[...], NT, preferred_element_type=jnp.float32
    )


def interior_block(rows, slab_potential, table):
    count, length = rows.shape
    step = count // 2
    return pl.pallas_call(
        interior_kernel,
        grid=(2,),
        in_specs=[
            pl.BlockSpec((count, length), lambda i: (0, 0)),
            pl.BlockSpec((step, length), lambda i: (i, 0)),
            pl.BlockSpec((1, length), lambda i: (0, 0)),
            pl.BlockSpec(table.shape, lambda i: (0, 0, 0)),
        ],
        out_specs=pl.BlockSpec((step, count), lambda i: (i, 0)),
        out_shape=jax.ShapeDtypeStruct((count, count), jnp.float32),
        scratch_shapes=[
            pltpu.VMEM((step, padded_width(length)), jnp.bfloat16),
            pltpu.VMEM((step, length), jnp.bfloat16),
        ],
        compiler_params=pltpu.CompilerParams(vmem_limit_bytes=VMEM_LIMIT),
    )(rows, rows, (6.0 + slab_potential)[None], table)


def partials_kernel(inner_ref, near_ref, far_ref, lz_ref, rz_ref, ly_ref, ry_ref, out_ref):
    def product(a, b):
        return lax.dot_general(a, b, NT, preferred_element_type=jnp.float32)

    seam = product(near_ref[...], far_ref[...])
    out_ref[0] = ((inner_ref[...] - seam) * (1.0 / G)).astype(jnp.bfloat16)
    weight = -0.5 / PLANE
    out_ref[1] = (product(lz_ref[...], rz_ref[...]) * weight).astype(jnp.bfloat16)
    out_ref[2] = (product(ly_ref[...], ry_ref[...]) * weight).astype(jnp.bfloat16)


def partial_blocks(inner, near, far, lz, rz, ly, ry):
    count = inner.shape[0]
    step = count // 4

    def cut(value):
        return pl.BlockSpec((step, value.shape[1]), lambda i: (i, 0))

    def full(value):
        return pl.BlockSpec(value.shape, lambda i: (0, 0))

    return pl.pallas_call(
        partials_kernel,
        grid=(4,),
        in_specs=[cut(inner), cut(near), full(far), cut(lz), full(rz), cut(ly), full(ry)],
        out_specs=pl.BlockSpec((3, step, count), lambda i: (0, i, 0)),
        out_shape=jax.ShapeDtypeStruct((3, count, count), jnp.bfloat16),
        compiler_params=pltpu.CompilerParams(vmem_limit_bytes=VMEM_LIMIT),
    )(inner, near, far, lz, rz, ly, ry)


def apply_blocks(terms, current):
    offsets = [0, 1, -1, EB, -EB]
    running = jnp.zeros((terms[0][0].shape[0], current.shape[1]), jnp.float32)
    for position, offset in enumerate(offsets):
        matrix, contract = terms[position]
        if offset == 0:
            source = current
        else:
            source = from_behind(current, "elem", -offset)
        running = running + lax.dot_general(
            matrix, source, (((contract,), (0,)), ((), ())), preferred_element_type=jnp.float32
        )
    return running


def scaled(terms, current):
    return (apply_blocks(terms, current) - SHIFT_CENTER * current.astype(jnp.float32)) / HALF_WIDTH


def reduce_kernel(
    slabs, elements, part_ref, out_ref, mirror_ref, slots, sum_s, sum_r, gather_s, gather_r, mirror_s, mirror_r
):
    me, element = lax.axis_index("band"), lax.axis_index("elem")
    share = part_ref.shape[1] // slabs
    half = share // 2

    def along(axis, place, by, count):
        return {axis: lax.rem(place + by + count, count)}

    def rows(steps, ring):
        chunk = lax.rem(me + steps + 2 * slabs, slabs)
        return pl.ds(pl.multiple_of(chunk * share + ring * half, half), half)

    def copy(source, target, send, receive, device):
        return pltpu.make_async_remote_copy(
            src_ref=source,
            dst_ref=target,
            send_sem=send,
            recv_sem=receive,
            device_id=device,
            device_id_type=pl.DeviceIdType.MESH,
        )

    barrier = pltpu.get_barrier_semaphore()
    for axis, place, by, count in (
        ("band", me, 1, slabs),
        ("band", me, -1, slabs),
        ("elem", element, -1, elements),
        ("elem", element, -EB, elements),
    ):
        pl.semaphore_signal(
            barrier,
            inc=1,
            device_id=along(axis, place, by, count),
            device_id_type=pl.DeviceIdType.MESH,
        )
    pl.semaphore_wait(barrier, 4)

    sent = []
    ways = (1, -1)
    for step in range(slabs - 1):
        moving = []
        for ring, way in enumerate(ways):
            source = slots.at[ring, step - 1] if step else part_ref.at[:, rows(-way, ring), :]
            moving.append(
                copy(
                    source,
                    slots.at[ring, step],
                    sum_s.at[ring, step],
                    sum_r.at[ring, step],
                    along("band", me, way, slabs),
                )
            )
            moving[-1].start()
        for ring, way in enumerate(ways):
            moving[ring].wait_recv()
            place = rows(-way * (step + 2), ring)
            total = slots[ring, step].astype(jnp.float32) + part_ref[:, place, :].astype(jnp.float32)
            if step < slabs - 2:
                slots[ring, step] = total.astype(jnp.bfloat16)
            else:
                out_ref[:, place, :] = total.astype(jnp.bfloat16)
        sent += moving

    mirrors = []

    def hand_on(step, ring, way):
        place = rows(-way * step, ring)
        for which, by in enumerate((1, EB)):
            mirrors.append(
                copy(
                    out_ref.at[which + 1, place, :],
                    mirror_ref.at[which, place, :],
                    mirror_s.at[ring, step, which],
                    mirror_r.at[ring, step, which],
                    along("elem", element, by, elements),
                )
            )
            mirrors[-1].start()

    for step in range(slabs - 1):
        moving = []
        for ring, way in enumerate(ways):
            place = rows(-way * step, ring)
            moving.append(
                copy(
                    out_ref.at[:, place, :],
                    out_ref.at[:, place, :],
                    gather_s.at[ring, step],
                    gather_r.at[ring, step],
                    along("band", me, way, slabs),
                )
            )
            moving[-1].start()
        for ring, way in enumerate(ways):
            hand_on(step, ring, way)
        for ring in range(2):
            moving[ring].wait_recv()
        sent += moving
    for ring, way in enumerate(ways):
        hand_on(slabs - 1, ring, way)
    for one in sent:
        one.wait_send()
    for one in mirrors:
        one.wait()


def summed_blocks(partials):
    slabs, elements = lax.axis_size("band"), lax.axis_size("elem")
    kinds, count, width = partials.shape
    half = count // slabs // 2
    whole = pl.BlockSpec(memory_space=pltpu.VMEM)
    return pl.pallas_call(
        functools.partial(reduce_kernel, slabs, elements),
        in_specs=[whole],
        out_specs=[whole, whole],
        out_shape=[
            jax.ShapeDtypeStruct(partials.shape, jnp.bfloat16),
            jax.ShapeDtypeStruct((kinds - 1, count, width), jnp.bfloat16),
        ],
        scratch_shapes=[
            pltpu.VMEM((2, slabs - 1, kinds, half, width), jnp.bfloat16),
            pltpu.SemaphoreType.DMA((2, slabs - 1)),
            pltpu.SemaphoreType.DMA((2, slabs - 1)),
            pltpu.SemaphoreType.DMA((2, slabs - 1)),
            pltpu.SemaphoreType.DMA((2, slabs - 1)),
            pltpu.SemaphoreType.DMA((2, slabs, kinds - 1)),
            pltpu.SemaphoreType.DMA((2, slabs, kinds - 1)),
        ],
        compiler_params=pltpu.CompilerParams(
            collective_id=0, has_side_effects=True, vmem_limit_bytes=VMEM_LIMIT
        ),
    )(partials)


def on_device(orbitals, potential, basis_count, states):
    per_device = orbitals.shape[1]
    slabs = lax.axis_size("band")
    band_place = lax.axis_index("band")
    table = stencil_tables()
    start_index = band_place * per_device
    basis = filtered_basis(orbitals[0], potential[0], basis_count[0], start_index, slabs, table)
    basis_rows = lax.all_to_all(basis, "band", split_axis=0, concat_axis=0, tiled=True)
    basis_rows = basis_rows.reshape(slabs * per_device, -1)
    slab_length = basis_rows.shape[1]
    slab_potential = lax.dynamic_slice_in_dim(
        potential[0], band_place * slab_length, slab_length, 0
    )
    half = PLANE // 2
    initial, last = basis_rows[:, :PLANE], basis_rows[:, slab_length - PLANE :]
    up = [(i, i + 1) for i in range(slabs - 1)]
    down = [(j, i) for i, j in up]
    after = lax.ppermute(initial[:, :half], "band", down)
    before = lax.ppermute(last[:, half:], "band", up)
    lz, rz, ly, ry = face_layers(basis_rows)
    rz = from_behind(rz, "elem", -1)
    ry = from_behind(ry, "elem", -EB)
    inner = interior_block(basis_rows, slab_potential, table)
    near = jnp.concatenate([last[:, :half], after, initial[:, half:], before], axis=1)
    far = jnp.concatenate([after, last[:, :half], before, initial[:, half:]], axis=1)
    partials = partial_blocks(inner, near, far, lz, rz, ly, ry)
    summed, mirrored = summed_blocks(partials)
    terms = [(summed[0], 1), (summed[1], 1), (mirrored[0], 0), (summed[2], 1), (mirrored[1], 0)]
    start_states = states[0]
    first_term = scaled(terms, start_states).astype(jnp.bfloat16)
    second_term = (2.0 * scaled(terms, first_term) - start_states.astype(jnp.float32)).astype(
        jnp.bfloat16
    )
    third_term = 2.0 * scaled(terms, second_term) - first_term.astype(jnp.float32)
    magnitude = jnp.sqrt(jnp.mean(third_term * third_term, axis=0, keepdims=True) + 1e-06)
    return (third_term / magnitude).astype(jnp.bfloat16)[None]


def solution(mesh):
    placed = (P("elem", "band", None), P("elem", None), P("elem"), P("elem", None, "band"))
    return jax.shard_map(
        on_device, mesh=mesh, in_specs=placed, out_specs=P("elem", None, "band"), check_vma=False
    )
```

```python
import functools

import jax
import jax.numpy as jnp
from jax import lax
from jax.experimental import pallas as pl
from jax.experimental.pallas import tpu as pltpu
from jax.sharding import PartitionSpec as P
import ml_dtypes
import numpy as np

P_SIZE = 24
G = 13824
EB = 4
PLANE = P_SIZE * P_SIZE
PAD = 640
TILE = 256
PERIOD = 9
SPANS = ((-640, -256), (-128, 384), (512, 896))


LOW_EDGE = 4.0
HIGH_EDGE = 14.0
SHIFT_CENTER = 4.0
HALF_WIDTH = 6.0
VMEM_LIMIT = 48 * 1024 * 1024
NT = (((1,), (1,)), ((), ()))


def from_behind(value, axis, by):
    devices = lax.axis_size(axis)
    return lax.ppermute(value, axis, [(i, (i + by) % devices) for i in range(devices)])


def stencil_tables():
    tables = []
    source = np.concatenate([np.arange(*span) for span in SPANS])[:, None]
    for which in range(PERIOD):
        column = np.arange(TILE)[None]
        zpos = (which * TILE + column) % P_SIZE
        ypos = (which * TILE + column) // P_SIZE % P_SIZE
        hit = (source == column + PLANE) | (source == column - PLANE)
        hit = hit | ((source == column + 1) & (zpos < P_SIZE - 1))
        hit = hit | ((source == column - 1) & (zpos > 0))
        hit = hit | ((source == column + P_SIZE) & (ypos < P_SIZE - 1))
        hit = hit | ((source == column - P_SIZE) & (ypos > 0))
        tables.append(hit)
    return jnp.asarray(np.stack(tables).astype(ml_dtypes.bfloat16))


def padded_width(length):
    return 2 * PAD + (length + TILE - 1) // TILE * TILE


def windows(ref, at):
    parts = []
    for low, high in SPANS:
        start = PAD + at + low
        if not isinstance(at, int):
            start = pl.multiple_of(start, 128)
        parts.append(ref[:, pl.ds(start, high - low)])
    return jnp.concatenate(parts, axis=1)


def clear_pads(ref, length):
    ref[:, 0:PAD] = jnp.zeros((ref.shape[0], PAD), ref.dtype)
    inner = PAD + length // 128 * 128
    ref[:, inner:] = jnp.zeros((ref.shape[0], ref.shape[1] - inner), ref.dtype)


def filter_kernel(slabs, bounds_ref, orbitals_ref, diag_ref, table_ref, out_ref, low_ref, mid_ref, wide_ref):
    spread = 0.5 * (HIGH_EDGE - LOW_EDGE)
    rows, length = orbitals_ref.shape
    turn = PERIOD * TILE
    repeats = length // turn
    clear_pads(low_ref, length)
    clear_pads(mid_ref, length)
    low_ref[:, PAD : PAD + length] = orbitals_ref[...]

    def sums(ref, which):
        offset = which * TILE
        left = jnp.concatenate([windows(ref, offset + turn * r) for r in range(repeats)], axis=0)
        return jnp.dot(left, table_ref[which], preferred_element_type=jnp.float32)

    def tile_at(which, r):
        return pl.multiple_of(which * TILE + turn * r, TILE)

    @pl.loop(0, PERIOD)
    def _(which):
        total = sums(low_ref, which)
        for r in range(repeats):
            at = tile_at(which, r)
            value = diag_ref[0:1, pl.ds(at, TILE)] * orbitals_ref[:, pl.ds(at, TILE)].astype(
                jnp.float32
            ) - total[r * rows : (r + 1) * rows] * (1.0 / spread)
            wide_ref[:, pl.ds(at, TILE)] = value
            mid_ref[:, pl.ds(pl.multiple_of(PAD + at, 128), TILE)] = value.astype(jnp.bfloat16)

    def second(which, squares):
        total = sums(mid_ref, which)
        for r in range(repeats):
            at = tile_at(which, r)
            value = (
                2.0 * diag_ref[0:1, pl.ds(at, TILE)] * wide_ref[:, pl.ds(at, TILE)]
                - total[r * rows : (r + 1) * rows] * (2.0 / spread)
                - orbitals_ref[:, pl.ds(at, TILE)].astype(jnp.float32)
            )
            wide_ref[:, pl.ds(at, TILE)] = value
            squares = squares + value * value
        return squares

    squares = lax.fori_loop(0, PERIOD, second, jnp.zeros((rows, TILE), jnp.float32))
    squares = jnp.sum(squares, axis=1, keepdims=True)
    scale = 1.0 / jnp.sqrt(squares * (1.0 / length) + 1e-06)
    row = bounds_ref[1] + lax.broadcasted_iota(jnp.int32, (rows, 1), 0)
    scale = jnp.where(row < bounds_ref[0], scale, 0.0)
    share = length // slabs
    for slab in range(slabs):
        out_ref[slab] = (wide_ref[:, slab * share : (slab + 1) * share] * scale).astype(jnp.bfloat16)


def filtered_basis(orbitals, potential, kept_count, start_index, slabs, table):
    count, length = orbitals.shape
    middle = 0.5 * (HIGH_EDGE + LOW_EDGE)
    spread = 0.5 * (HIGH_EDGE - LOW_EDGE)
    diag = ((6.0 - middle) + potential)[None] / spread
    bounds = jnp.stack([kept_count, start_index]).astype(jnp.int32)
    whole = pl.BlockSpec(memory_space=pltpu.VMEM)
    return pl.pallas_call(
        functools.partial(filter_kernel, slabs),
        in_specs=[pl.BlockSpec(memory_space=pltpu.SMEM), whole, whole, whole],
        out_specs=whole,
        out_shape=jax.ShapeDtypeStruct((slabs, count, length // slabs), jnp.bfloat16),
        scratch_shapes=[
            pltpu.VMEM((count, padded_width(length)), jnp.bfloat16),
            pltpu.VMEM((count, padded_width(length)), jnp.bfloat16),
            pltpu.VMEM((count, length), jnp.float32),
        ],
        compiler_params=pltpu.CompilerParams(vmem_limit_bytes=VMEM_LIMIT),
    )(bounds, orbitals, diag, table)


def face_chunk(length):
    return 1152 if length % 1152 == 0 else length


def face_selector(chunk):
    points = chunk // P_SIZE
    group = (2 * points + 127) // 128 * 128
    where = np.arange(chunk)[:, None]
    zpos, ypos, xpos = where % P_SIZE, where // P_SIZE % P_SIZE, where // PLANE
    column = np.arange(group)[None]
    point, late = column % points, column >= points
    used = column < 2 * points
    top = P_SIZE - 1
    layers = [(top - 1, top), (0, 1)]
    parts = []
    for pos, spot in ((zpos, where // P_SIZE), (ypos, xpos * P_SIZE + zpos)):
        for early_layer, late_layer in layers:
            layer = np.where(late, late_layer, early_layer)
            parts.append(((spot == point) & (pos == layer) & used))
    return jnp.asarray(np.concatenate(parts, axis=1).astype(ml_dtypes.bfloat16))


def blocks_kernel(
    slabs,
    elements,
    rows_ref,
    diag_ref,
    table_ref,
    select_ref,
    out_ref,
    mirror_ref,
    wide_ref,
    applied_ref,
    inner_ref,
    part_ref,
    seam_refs,
    face_refs,
    slots,
    seam_s,
    seam_r,
    face_s,
    face_r,
    sum_s,
    sum_r,
    gather_s,
    gather_r,
    mirror_s,
    mirror_r,
):
    me, element = lax.axis_index("band"), lax.axis_index("elem")
    share = part_ref.shape[1] // slabs
    half = share // 2
    functions, length = rows_ref.shape
    last_ref, first_ref, up_ref, down_ref, after_ref, before_ref = seam_refs
    lz_ref, rz_ref, ly_ref, ry_ref, rz_in, ry_in = face_refs

    def along(axis, place, by, count):
        return {axis: lax.rem(place + by + count, count)}

    def rows(steps, ring):
        chunk = lax.rem(me + steps + 2 * slabs, slabs)
        return pl.ds(pl.multiple_of(chunk * share + ring * half, half), half)

    def copy(source, target, send, receive, device):
        return pltpu.make_async_remote_copy(
            src_ref=source,
            dst_ref=target,
            send_sem=send,
            recv_sem=receive,
            device_id=device,
            device_id_type=pl.DeviceIdType.MESH,
        )

    barrier = pltpu.get_barrier_semaphore()
    for axis, place, by, count in (
        ("band", me, 1, slabs),
        ("band", me, -1, slabs),
        ("elem", element, -1, elements),
        ("elem", element, -EB, elements),
        ("elem", element, 1, elements),
        ("elem", element, EB, elements),
    ):
        pl.semaphore_signal(
            barrier,
            inc=1,
            device_id=along(axis, place, by, count),
            device_id_type=pl.DeviceIdType.MESH,
        )
    pl.semaphore_wait(barrier, 6)

    seam = PLANE // 2
    down_ref[...] = rows_ref[:, 0:seam]
    first_ref[...] = rows_ref[:, seam:PLANE]
    last_ref[...] = rows_ref[:, length - PLANE : length - seam]
    up_ref[...] = rows_ref[:, length - seam : length]
    downward = copy(
        down_ref, after_ref, seam_s.at[0], seam_r.at[0], along("band", me, -1, slabs)
    )
    upward = copy(up_ref, before_ref, seam_s.at[1], seam_r.at[1], along("band", me, 1, slabs))

    @pl.when(me > 0)
    def _():
        downward.start()

    @pl.when(me < slabs - 1)
    def _():
        upward.start()

    chunk = select_ref.shape[0]
    group = select_ref.shape[1] // 4
    block = functions // 2

    @pl.loop(0, 2)
    def _(index):
        here = pl.ds(pl.multiple_of(index * block, block), block)
        for which in range(length // chunk):
            picked = jnp.dot(
                rows_ref[here, which * chunk : (which + 1) * chunk],
                select_ref[...],
                preferred_element_type=jnp.float32,
            ).astype(jnp.bfloat16)
            for place, face in enumerate((lz_ref, rz_ref, ly_ref, ry_ref)):
                face[here, which * group : (which + 1) * group] = picked[
                    :, place * group : (place + 1) * group
                ]

    faces = [
        copy(rz_ref, rz_in, face_s.at[0], face_r.at[0], along("elem", element, -1, elements)),
        copy(ry_ref, ry_in, face_s.at[1], face_r.at[1], along("elem", element, -EB, elements)),
    ]
    for one in faces:
        one.start()

    clear_pads(wide_ref, length)
    wide_ref[:, PAD : PAD + length] = rows_ref[...]

    @pl.loop(0, 2)
    def _(index):
        here = pl.ds(pl.multiple_of(index * block, block), block)
        view = wide_ref.at[here]
        for at in range(0, length, TILE):
            size = min(TILE, length - at)
            total = jnp.dot(
                windows(view, at), table_ref[at // TILE % PERIOD], preferred_element_type=jnp.float32
            )
            applied_ref[:, at : at + size] = (
                diag_ref[0:1, at : at + size] * rows_ref[here, at : at + size].astype(jnp.float32)
                - total[:, :size]
            ).astype(jnp.bfloat16)
        inner_ref[here, :] = lax.dot_general(
            applied_ref[...], rows_ref[...], NT, preferred_element_type=jnp.float32
        )

    def product(a, b):
        return lax.dot_general(a, b, NT, preferred_element_type=jnp.float32)

    @pl.when(me < slabs - 1)
    def _():
        downward.wait_recv()

    @pl.when(me == slabs - 1)
    def _():
        after_ref[...] = jnp.zeros(after_ref.shape, jnp.bfloat16)

    @pl.when(me > 0)
    def _():
        upward.wait_recv()

    @pl.when(me == 0)
    def _():
        before_ref[...] = jnp.zeros(before_ref.shape, jnp.bfloat16)

    for one in faces:
        one.wait_recv()
    weight = -0.5 / PLANE

    @pl.loop(0, 2)
    def _(index):
        here = pl.ds(pl.multiple_of(index * block, block), block)
        joined = product(last_ref[here, :], after_ref[...]) + product(after_ref[here, :], last_ref[...])
        joined = joined + product(first_ref[here, :], before_ref[...])
        joined = joined + product(before_ref[here, :], first_ref[...])
        part_ref[0, here, :] = ((inner_ref[here, :] - joined) * (1.0 / G)).astype(jnp.bfloat16)
        part_ref[1, here, :] = (product(lz_ref[here, :], rz_in[...]) * weight).astype(jnp.bfloat16)
        part_ref[2, here, :] = (product(ly_ref[here, :], ry_in[...]) * weight).astype(jnp.bfloat16)

    sent = []
    ways = (1, -1)
    for step in range(slabs - 1):
        moving = []
        for ring, way in enumerate(ways):
            source = slots.at[ring, step - 1] if step else part_ref.at[:, rows(-way, ring), :]
            moving.append(
                copy(
                    source,
                    slots.at[ring, step],
                    sum_s.at[ring, step],
                    sum_r.at[ring, step],
                    along("band", me, way, slabs),
                )
            )
            moving[-1].start()
        for ring, way in enumerate(ways):
            moving[ring].wait_recv()
            place = rows(-way * (step + 2), ring)
            total = slots[ring, step].astype(jnp.float32) + part_ref[:, place, :].astype(jnp.float32)
            if step < slabs - 2:
                slots[ring, step] = total.astype(jnp.bfloat16)
            else:
                out_ref[:, place, :] = total.astype(jnp.bfloat16)
        sent += moving

    mirrors = []

    def hand_on(step, ring, way):
        place = rows(-way * step, ring)
        for which, by in enumerate((1, EB)):
            mirrors.append(
                copy(
                    out_ref.at[which + 1, place, :],
                    mirror_ref.at[which, place, :],
                    mirror_s.at[ring, step, which],
                    mirror_r.at[ring, step, which],
                    along("elem", element, by, elements),
                )
            )
            mirrors[-1].start()

    for step in range(slabs - 1):
        moving = []
        for ring, way in enumerate(ways):
            place = rows(-way * step, ring)
            moving.append(
                copy(
                    out_ref.at[:, place, :],
                    out_ref.at[:, place, :],
                    gather_s.at[ring, step],
                    gather_r.at[ring, step],
                    along("band", me, way, slabs),
                )
            )
            moving[-1].start()
        for ring, way in enumerate(ways):
            hand_on(step, ring, way)
        for ring in range(2):
            moving[ring].wait_recv()
        sent += moving
    for ring, way in enumerate(ways):
        hand_on(slabs - 1, ring, way)
    for one in sent + faces:
        one.wait_send()

    @pl.when(me > 0)
    def _():
        downward.wait_send()

    @pl.when(me < slabs - 1)
    def _():
        upward.wait_send()

    for one in mirrors:
        one.wait()


def summed_blocks(rows, slab_potential, table):
    slabs, elements = lax.axis_size("band"), lax.axis_size("elem")
    count, length = rows.shape
    half = count // slabs // 2
    chunk = face_chunk(length)
    select = face_selector(chunk)
    width = length // chunk * (select.shape[1] // 4)
    whole = pl.BlockSpec(memory_space=pltpu.VMEM)
    dma = pltpu.SemaphoreType.DMA
    return pl.pallas_call(
        functools.partial(blocks_kernel, slabs, elements),
        in_specs=[whole] * 4,
        out_specs=[whole, whole],
        out_shape=[
            jax.ShapeDtypeStruct((3, count, count), jnp.bfloat16),
            jax.ShapeDtypeStruct((2, count, count), jnp.bfloat16),
        ],
        scratch_shapes=[
            pltpu.VMEM((count, padded_width(length)), jnp.bfloat16),
            pltpu.VMEM((count // 2, length), jnp.bfloat16),
            pltpu.VMEM((count, count), jnp.float32),
            pltpu.VMEM((3, count, count), jnp.bfloat16),
            [pltpu.VMEM((count, PLANE // 2), jnp.bfloat16) for _ in range(6)],
            [pltpu.VMEM((count, width), jnp.bfloat16) for _ in range(6)],
            pltpu.VMEM((2, slabs - 1, 3, half, count), jnp.bfloat16),
            dma((2,)),
            dma((2,)),
            dma((2,)),
            dma((2,)),
            dma((2, slabs - 1)),
            dma((2, slabs - 1)),
            dma((2, slabs - 1)),
            dma((2, slabs - 1)),
            dma((2, slabs, 2)),
            dma((2, slabs, 2)),
        ],
        compiler_params=pltpu.CompilerParams(
            collective_id=0, has_side_effects=True, vmem_limit_bytes=VMEM_LIMIT
        ),
    )(rows, (6.0 + slab_potential)[None], table, select)


def apply_blocks(terms, current):
    offsets = [0, 1, -1, EB, -EB]
    running = jnp.zeros((terms[0][0].shape[0], current.shape[1]), jnp.float32)
    for position, offset in enumerate(offsets):
        matrix, contract = terms[position]
        if offset == 0:
            source = current
        else:
            source = from_behind(current, "elem", -offset)
        running = running + lax.dot_general(
            matrix, source, (((contract,), (0,)), ((), ())), preferred_element_type=jnp.float32
        )
    return running


def scaled(terms, current):
    return (apply_blocks(terms, current) - SHIFT_CENTER * current.astype(jnp.float32)) / HALF_WIDTH


def on_device(orbitals, potential, basis_count, states):
    per_device = orbitals.shape[1]
    slabs = lax.axis_size("band")
    band_place = lax.axis_index("band")
    table = stencil_tables()
    start_index = band_place * per_device
    basis = filtered_basis(orbitals[0], potential[0], basis_count[0], start_index, slabs, table)
    basis_rows = lax.all_to_all(basis, "band", split_axis=0, concat_axis=0, tiled=True)
    basis_rows = basis_rows.reshape(slabs * per_device, -1)
    slab_length = basis_rows.shape[1]
    slab_potential = lax.dynamic_slice_in_dim(
        potential[0], band_place * slab_length, slab_length, 0
    )
    summed, mirrored = summed_blocks(basis_rows, slab_potential, table)
    terms = [(summed[0], 1), (summed[1], 1), (mirrored[0], 0), (summed[2], 1), (mirrored[1], 0)]
    start_states = states[0]
    first_term = scaled(terms, start_states).astype(jnp.bfloat16)
    second_term = (2.0 * scaled(terms, first_term) - start_states.astype(jnp.float32)).astype(
        jnp.bfloat16
    )
    third_term = 2.0 * scaled(terms, second_term) - first_term.astype(jnp.float32)
    magnitude = jnp.sqrt(jnp.mean(third_term * third_term, axis=0, keepdims=True) + 1e-06)
    return (third_term / magnitude).astype(jnp.bfloat16)[None]


def solution(mesh):
    placed = (P("elem", "band", None), P("elem", None), P("elem"), P("elem", None, "band"))
    return jax.shard_map(
        on_device, mesh=mesh, in_specs=placed, out_specs=P("elem", None, "band"), check_vma=False
    )
```
